32 devices in a mesh: noise: 4 (over z), dp: 8 (over y, x, core).
Axes of the slice: x: 2, y: 2, z: 4, core: 2. Of those that a mesh axis runs over, the one named last changes fastest.
Arguments:
- noise_points: float32 [6144, 512], P('noise'), may hold values from -1.5 to 1.5
- data_points: float32 [3072, 512], P('dp', 'noise'), may hold values from -1.5 to 1.5
- noise_blocks: int32 [4], P('noise'), may hold values from 1 to 12, as said below
- data_blocks: int32 [8], P('dp'), may hold values from 1 to 3, as said below
Outputs:
- noise_potential: float32 [6144], P('noise')
- data_potential: float32 [3072], P('dp')
- noise_target: float32 [512, 6144], P('dp', 'noise')
- data_target: float32 [512, 3072], P('noise', 'dp')
The draws below stay inside these ranges and needn't reach their ends.
Inputs may be any that keep to these rules, and one draw needn't show every extreme that they name: `noise_blocks`: blocks 0 up to this count of each device's 12 slots are live, the rest padding; some device has all 12 live. `data_blocks`: blocks 0 up to this count of each device's 3 slots are live, the rest padding; some device has all 3 live.
All inputs are finite; a program needn't handle non-finite values.
Results may differ from the reference program's by a relative error of at most 0.0003.
Values sent between devices are 32-bit elements; how exact they have to be, the bound alone decides.
A program may use at most 64 MiB of HBM per device.

```python
import jax
import jax.numpy as jnp
from jax import lax

P_SIZE = 512
BLOCK = 128
XB_DEV = 12
YB_DEV = 3
ITERS = 3
NX = 6144
NY = 3072


def point_pair(key):
    base = jax.random.fold_in(key, 4242)
    key_noise, key_data = jax.random.split(base, 2)
    rows_dev = XB_DEV * BLOCK
    cols_dev = YB_DEV * BLOCK
    groups = NX // rows_dev
    data_groups = NY // cols_dev
    noise = jax.random.normal(key_noise, (NX, P_SIZE), jnp.float32) * 0.125
    data = jax.random.normal(key_data, (NY, P_SIZE), jnp.float32) * 0.125
    far_rows = jnp.arange(groups, dtype=jnp.int32) * rows_dev + 2
    far_cols = jnp.arange(data_groups, dtype=jnp.int32) * cols_dev + 2
    row_strength = 14.0 + 7.0 * (jnp.arange(groups, dtype=jnp.int32) % 3).astype(jnp.float32)
    col_strength = 14.0 + 7.0 * (jnp.arange(data_groups, dtype=jnp.int32) % 3).astype(jnp.float32)
    noise = noise.at[far_rows].add(jnp.sqrt(row_strength / P_SIZE)[:, None])
    data = data.at[far_cols].add(-jnp.sqrt(col_strength / P_SIZE)[:, None])
    return (jnp.clip(noise, -1.5, 1.5), jnp.clip(data, -1.5, 1.5))


def draw_noise_points(key, part):
    return point_pair(key)[0]


def draw_data_points(key, part):
    return point_pair(key)[1]


def block_counts(key, count, most):
    key_base, key_full = jax.random.split(key, 2)
    counts = jax.random.randint(key_base, (count,), 1, most // 2 + 1, jnp.int32)
    full = jax.random.randint(key_full, (), 0, count, jnp.int32)
    return counts.at[full].set(most)


def draw_noise_blocks(key, part):
    return block_counts(jax.random.fold_in(key, 11), NX // (XB_DEV * BLOCK), XB_DEV)


def draw_data_blocks(key, part):
    return block_counts(jax.random.fold_in(key, 13), NY // (YB_DEV * BLOCK), YB_DEV)


def setup_inputs(seed: int = 0) -> dict:
    key_of = jax.random.split(jax.random.key(seed), 5)
    noise_points = draw_noise_points(jax.random.fold_in(key_of[4], 71), 0)
    data_points = draw_data_points(jax.random.fold_in(key_of[4], 71), 0)
    noise_blocks = draw_noise_blocks(jax.random.fold_in(key_of[4], 71), 0)
    data_blocks = draw_data_blocks(jax.random.fold_in(key_of[4], 71), 0)
    return {"noise_points": noise_points, "data_points": data_points, "noise_blocks": noise_blocks, "data_blocks": data_blocks}


SMOOTHING_TEMP = 0.125


def pair_cost(rows, cols, col_sq):
    row_sq = jnp.sum(rows * rows, axis=1)
    cross = jnp.dot(rows, cols.T, precision=lax.Precision.HIGHEST, preferred_element_type=jnp.float32)
    return row_sq[:, None] + col_sq[None, :] - 2.0 * cross


def reference(noise_points, data_points, noise_blocks, data_blocks):
    rows_dev = XB_DEV * BLOCK
    cols_dev = YB_DEV * BLOCK
    groups = NX // rows_dev
    log_noise_mass = -jnp.log((jnp.sum(noise_blocks) * BLOCK).astype(jnp.float32))
    log_data_mass = -jnp.log((jnp.sum(data_blocks) * BLOCK).astype(jnp.float32))
    row_limit = jnp.repeat((noise_blocks * BLOCK).astype(jnp.int32), rows_dev, total_repeat_length=NX)
    col_limit = jnp.repeat((data_blocks * BLOCK).astype(jnp.int32), cols_dev, total_repeat_length=NY)
    row_active = (jnp.arange(NX, dtype=jnp.int32) % rows_dev) < row_limit
    column_active = (jnp.arange(NY, dtype=jnp.int32) % cols_dev) < col_limit
    grouped = noise_points.reshape(groups, rows_dev, P_SIZE)
    live_grouped = row_active.reshape(groups, rows_dev)
    col_sq = jnp.sum(data_points * data_points, axis=1)

    def row_scores(points, data_potential):
        transport_cost = pair_cost(points, data_points, col_sq)
        return jnp.where(column_active[None, :], (data_potential[None, :] - transport_cost) / SMOOTHING_TEMP + log_data_mass, -jnp.inf)

    def row_threshold(data_potential):
        def one(points):
            pair_scores = row_scores(points, data_potential)
            peak = jnp.max(pair_scores, axis=1)
            return peak + jnp.log(jnp.sum(jnp.exp(pair_scores - peak[:, None]), axis=1))
        return lax.map(one, grouped).reshape(NX)

    def column_level(noise_potential):
        duals = noise_potential.reshape(groups, rows_dev)

        def step(carry, items):
            peak, mass = carry
            points, active_pairs, dual_value = items
            transport_cost = pair_cost(points, data_points, col_sq)
            pair_scores = jnp.where(active_pairs[:, None], (dual_value[:, None] - transport_cost) / SMOOTHING_TEMP + log_noise_mass, -jnp.inf)
            top = jnp.maximum(peak, jnp.max(pair_scores, axis=0))
            mass = mass * jnp.exp(peak - top) + jnp.sum(jnp.exp(pair_scores - top[None, :]), axis=0)
            return (top, mass), None

        init = (jnp.full((NY,), -jnp.inf, jnp.float32), jnp.zeros((NY,), jnp.float32))
        (peak, mass), _ = lax.scan(step, init, (grouped, live_grouped, duals))
        return peak + jnp.log(mass)

    data_potential = jnp.zeros((NY,), jnp.float32)
    noise_potential = jnp.zeros((NX,), jnp.float32)
    for turn in range(ITERS):
        noise_potential = jnp.where(row_active, -SMOOTHING_TEMP * row_threshold(data_potential), 0.0)
        data_potential = jnp.where(column_active, -SMOOTHING_TEMP * column_level(noise_potential), 0.0)

    def project_rows(items):
        points, active_pairs = items
        pair_scores = row_scores(points, data_potential)
        peak = jnp.max(pair_scores, axis=1)
        level = peak + jnp.log(jnp.sum(jnp.exp(pair_scores - peak[:, None]), axis=1))
        plan_weights = jnp.where(active_pairs[:, None] & column_active[None, :], jnp.exp(pair_scores - level[:, None]), 0.0)
        return jnp.dot(plan_weights, data_points, precision=lax.Precision.HIGHEST, preferred_element_type=jnp.float32)

    noise_target = lax.map(project_rows, (grouped, live_grouped)).reshape(NX, P_SIZE).T

    duals = noise_potential.reshape(groups, rows_dev)

    def project_cols(total, items):
        points, active_pairs, dual_value = items
        transport_cost = pair_cost(points, data_points, col_sq)
        plan_weights = jnp.where(active_pairs[:, None] & column_active[None, :], jnp.exp((dual_value[:, None] + data_potential[None, :] - transport_cost) / SMOOTHING_TEMP + log_noise_mass), 0.0)
        total = total + jnp.dot(plan_weights.T, points, precision=lax.Precision.HIGHEST, preferred_element_type=jnp.float32)
        return total, None

    summed, _ = lax.scan(project_cols, jnp.zeros((NY, P_SIZE), jnp.float32), (grouped, live_grouped, duals))
    return noise_potential, data_potential, noise_target, summed.T
```

```python
import functools

import jax
import jax.numpy as jnp
from jax import lax
from jax.experimental import pallas as pl
from jax.experimental.pallas import tpu as pltpu
from jax.sharding import PartitionSpec as P

BLOCK = 128
ITERS = 3
SMOOTHING_TEMP = 0.125
TILE = 256
MESH = pl.DeviceIdType.MESH
F32 = jnp.float32
BF16 = jnp.bfloat16
NT = (((1,), (1,)), ((), ()))


def split(x):
    hi = x.astype(BF16)
    return hi, (x - hi.astype(F32)).astype(BF16)


def dot3(ahi, alo, bhi, blo):
    d = functools.partial(jnp.dot, preferred_element_type=F32)
    return d(ahi, bhi) + (d(ahi, blo) + d(alo, bhi))


def kernel(n, nz, x_ref, y_ref, nb_ref, db_ref, f_ref, g_ref, nt_ref, dt_ref,
           dbuf, dfull, yt, kt, gmb, fmrow, facrow, xsq, xhi, xlo, whi, wlo, dhi, dlo,
           rst, cst, acc, rb, ptmp, pbuf, zbuf,
           ag_s, ag_r, rs_s, rs_r, cs_s, cs_r, h_s, h_r, z_s, z_r):
    me = lax.axis_index("dp")
    mz = lax.axis_index("noise")
    rows, coords = x_ref.shape
    cols, cz = y_ref.shape
    nr, nc = rows // BLOCK, cols // BLOCK
    cb = coords // n
    steps = n.bit_length() - 1

    barrier = pltpu.get_barrier_semaphore()
    for o in range(1, n):
        pl.semaphore_signal(barrier, inc=1, device_id={"dp": lax.rem(me + o, n)}, device_id_type=MESH)
    for o in range(1, nz):
        pl.semaphore_signal(barrier, inc=1, device_id={"noise": lax.rem(mz + o, nz)}, device_id_type=MESH)
    pl.semaphore_wait(barrier, n + nz - 2)

    def copy(src, dst, ssem, rsem, axis, to):
        return pltpu.make_async_remote_copy(
            src_ref=src, dst_ref=dst, send_sem=ssem, recv_sem=rsem,
            device_id={axis: to}, device_id_type=MESH)

    def spread(buf, ssem, rsem, axis, size, mine):
        sent = []
        for o in range(1, size):
            c = copy(buf.at[mine], buf.at[mine], ssem.at[o], rsem.at[mine], axis, lax.rem(mine + o, size))
            c.start()
            sent.append(c)
        return sent

    def arrive(buf, ssem, rsem, axis, size, mine):
        for o in range(1, size):
            src = lax.rem(mine + size - o, size)
            copy(buf.at[src], buf.at[src], ssem.at[o], rsem.at[src], axis, src).wait_recv()

    pending = []
    dbuf[mz] = y_ref[...]
    pending += spread(dbuf, ag_s, ag_r, "noise", nz, mz)

    ones = jnp.ones((8, coords), F32)

    def prep(t, _):
        at = pl.ds(pl.multiple_of(t * TILE, TILE), TILE)
        x = x_ref[at, :]
        hi, lo = split(x)
        xhi[at, :] = hi
        xlo[at, :] = lo
        xsq[:, at] = lax.dot_general(ones, x * x, NT, precision=lax.Precision.HIGHEST,
                                     preferred_element_type=F32)[0:1, :]
        return 0

    lax.fori_loop(0, rows // TILE, prep, 0)

    live_i = lax.broadcasted_iota(jnp.int32, (nr, BLOCK), 0) < nb_ref[0]
    live_j = lax.broadcasted_iota(jnp.int32, (nc, BLOCK), 0) < db_ref[0]
    eye = (lax.broadcasted_iota(jnp.int32, (BLOCK, BLOCK), 0)
           == lax.broadcasted_iota(jnp.int32, (BLOCK, BLOCK), 1))

    def set_gm(g):
        gm = jnp.where(live_j, g, -jnp.inf)
        for k in range(nc):
            gmb[k * BLOCK:(k + 1) * BLOCK, :] = jnp.broadcast_to(gm[k:k + 1, :], (BLOCK, BLOCK)).T

    set_gm(jnp.zeros((nc, BLOCK), F32))

    arrive(dbuf, ag_s, ag_r, "noise", nz, mz)
    for k in range(nz):
        dfull[:, k * cz:(k + 1) * cz] = dbuf[k]
    ysq = jnp.sum(dfull[...] * dfull[...], axis=1, keepdims=True)

    def cost(t, _):
        at = pl.ds(pl.multiple_of(t * TILE, TILE), TILE)
        cross = lax.dot_general(dfull[...], x_ref[at, :], NT, precision=lax.Precision.HIGHEST,
                                preferred_element_type=F32)
        kt[:, at] = (2.0 * cross - (xsq[:, at] + ysq)) * (1.0 / SMOOTHING_TEMP)
        return 0

    lax.fori_loop(0, rows // TILE, cost, 0)

    def row_pass(r, keep):
        def body(c, _):
            at = pl.ds(pl.multiple_of(c * BLOCK, BLOCK), BLOCK)
            s = kt[:, at] + gmb[...]
            top = jnp.max(s, axis=0, keepdims=True)
            e = jnp.exp(s - top)
            rst[r, me, pl.ds(c, 1), :] = top
            rst[r, me, pl.ds(nr + c, 1), :] = jnp.sum(e, axis=0, keepdims=True)
            if keep:
                hi, lo = split(e)
                whi[:, at] = hi
                wlo[:, at] = lo
            return 0

        lax.fori_loop(0, nr, body, 0)
        rst[r, me, 2 * nr:2 * nr + 8, :] = jnp.full((8, BLOCK), db_ref[0].astype(F32), F32)
        return spread(rst.at[r], rs_s.at[r], rs_r.at[r], "dp", n, me)

    def col_pass(r):
        def body(k, _):
            s = kt[pl.ds(pl.multiple_of(k * BLOCK, BLOCK), BLOCK), :] + fmrow[...]
            top = jnp.max(s, axis=1, keepdims=True)
            mass = jnp.sum(jnp.exp(s - top), axis=1, keepdims=True)
            cst[r, mz, pl.ds(k, 1), :] = jnp.sum(jnp.where(eye, top, 0.0), axis=0, keepdims=True)
            cst[r, mz, pl.ds(nc + k, 1), :] = jnp.sum(jnp.where(eye, mass, 0.0), axis=0, keepdims=True)
            return 0

        lax.fori_loop(0, nc, body, 0)
        cst[r, mz, 2 * nc:2 * nc + 1, :] = jnp.full((1, BLOCK), nb_ref[0].astype(F32), F32)
        return spread(cst.at[r], cs_s.at[r], cs_r.at[r], "noise", nz, mz)

    def combine(st, r, size, m):
        tops = [st[r, k, 0:m, :] for k in range(size)]
        top = functools.reduce(jnp.maximum, tops)
        mass = sum(st[r, k, m:2 * m, :] * jnp.exp(tops[k] - top) for k in range(size))
        return top + jnp.log(mass)

    def log_mass(st, size, m):
        count = sum(st[0, k, 2 * m:2 * m + 1, :] for k in range(size))
        return -jnp.log(count * float(BLOCK))

    def set_row(ref, v):
        for c in range(nr):
            ref[:, c * BLOCK:(c + 1) * BLOCK] = v[c:c + 1, :]

    log_a = log_b = f = g = None
    for turn in range(ITERS):
        pending += row_pass(turn, False)
        if turn == 0:
            full = dfull[...].T
            hi, lo = split(full)
            yt[0] = hi.astype(F32)
            yt[1] = lo.astype(F32)
        arrive(rst.at[turn], rs_s.at[turn], rs_r.at[turn], "dp", n, me)
        if turn == 0:
            log_b = log_mass(rst, n, nr)
        f = -(combine(rst, turn, n, nr) + log_b)
        set_row(fmrow, jnp.where(live_i, f, -jnp.inf))
        pending += col_pass(turn)
        arrive(cst.at[turn], cs_s.at[turn], cs_r.at[turn], "noise", nz, mz)
        if turn == 0:
            log_a = log_mass(cst, nz, nc)
        g = -(combine(cst, turn, nz, nc) + log_a)
        set_gm(g)
    f_ref[...] = jnp.where(live_i, SMOOTHING_TEMP * f, 0.0)
    g_ref[...] = jnp.where(live_j, SMOOTHING_TEMP * g, 0.0)

    pending += row_pass(ITERS, True)

    set_row(fmrow, jnp.where(live_i, f + log_a, -jnp.inf))

    def plan(c, _):
        at = pl.ds(pl.multiple_of(c * BLOCK, BLOCK), BLOCK)
        hi, lo = split(jnp.exp(kt[:, at] + fmrow[:, at] + gmb[...]))
        dhi[:, at] = hi
        dlo[:, at] = lo
        return 0

    lax.fori_loop(0, nr, plan, 0)

    def project(t, _):
        at = pl.ds(pl.multiple_of(t * TILE, TILE), TILE)
        ptmp[:, at] = dot3(dhi[...], dlo[...], xhi[:, at], xlo[:, at])
        return 0

    lax.fori_loop(0, coords // TILE, project, 0)
    for k in range(nz):
        pbuf[k] = ptmp[:, k * cz:(k + 1) * cz]
    for o in range(1, nz):
        to = lax.rem(mz + o, nz)
        c = copy(pbuf.at[to], zbuf.at[o], z_s.at[o], z_r.at[o], "noise", to)
        c.start()
        pending.append(c)

    arrive(rst.at[ITERS], rs_s.at[ITERS], rs_r.at[ITERS], "dp", n, me)
    level = combine(rst, ITERS, n, nr)
    set_row(facrow, jnp.where(live_i, jnp.exp(rst[ITERS, me, 0:nr, :] - level), 0.0))

    core = lax.rem(me, 2)

    def flip(w):
        return w * (1 - 2 * lax.rem(me // w, 2))

    delta = [flip(1)] + [(1 - core) * flip(1 << s) + core * flip(1 << (steps - s)) for s in range(1, steps)]

    def owner(q):
        d = me
        for s in range(steps):
            if (q >> s) & 1:
                d = d + delta[s]
        return d

    def landed(s, q):
        if s > 0:
            return q - (1 << s)
        return sum(1 << (steps - t) for t in range(1, steps) if (q >> t) & 1)

    slot = {}
    for s in range(steps):
        for q in range(0, n, 2 << s):
            slot[s, q] = len(slot)

    def half(odd):
        qs = list(range(odd, n, 2))
        hi = jnp.concatenate([yt[0, pl.ds(pl.multiple_of(owner(q) * cb, cb), cb), :] for q in qs], axis=0).astype(BF16)
        lo = jnp.concatenate([yt[1, pl.ds(pl.multiple_of(owner(q) * cb, cb), cb), :] for q in qs], axis=0).astype(BF16)

        def body(t, _):
            at = pl.ds(pl.multiple_of(t * TILE, TILE), TILE)
            out = dot3(hi, lo, whi[:, at], wlo[:, at]) * facrow[:, at]
            for m, q in enumerate(qs):
                acc[q, :, at] = out[m * cb:(m + 1) * cb, :]
            return 0

        lax.fori_loop(0, rows // TILE, body, 0)

    def hop(s, q):
        to = landed(s, q)
        return copy(acc.at[q], rb.at[slot[s, to]], h_s.at[q], h_r.at[slot[s, to]], "dp", me + delta[s])

    def take(s, q):
        copy(acc.at[q], rb.at[slot[s, q]], h_s.at[q], h_r.at[slot[s, q]], "dp", me + delta[s]).wait_recv()
        acc[q] += rb[slot[s, q]]

    half(1)
    for q in range(1, n, 2):
        c = hop(0, q)
        c.start()
        pending.append(c)
    half(0)
    for s in range(1, steps):
        for q in range(1 << s, n, 2 << s):
            take(s - 1, q)
            c = hop(s, q)
            c.start()
            pending.append(c)
        for q in range(0, n, 2 << s):
            take(s - 1, q)

    total = pbuf[mz]
    for o in range(1, nz):
        copy(pbuf.at[mz], zbuf.at[o], z_s.at[o], z_r.at[o], "noise", lax.rem(mz + o, nz)).wait_recv()
        total = total + zbuf[o]
    dt_ref[...] = total.T

    take(steps - 1, 0)
    nt_ref[...] = acc[0]
    for c in pending:
        c.wait_send()


def on_device(n, nz, x, y, nb, db):
    rows, coords = x.shape
    cols, cz = y.shape
    nr, nc = rows // BLOCK, cols // BLOCK
    cb = coords // n
    steps = n.bit_length() - 1
    crow = -(-(2 * nc + 1) // 8) * 8
    vm = pltpu.VMEM
    dma = lambda *s: pltpu.SemaphoreType.DMA(s)
    macs = rows * cols * coords
    f, g, nt, dt = pl.pallas_call(
        functools.partial(kernel, n, nz),
        out_shape=(
            jax.ShapeDtypeStruct((nr, BLOCK), F32),
            jax.ShapeDtypeStruct((nc, BLOCK), F32),
            jax.ShapeDtypeStruct((cb, rows), F32),
            jax.ShapeDtypeStruct((cz, cols), F32),
        ),
        in_specs=[pl.BlockSpec(memory_space=vm)] * 2 + [pl.BlockSpec(memory_space=pltpu.SMEM)] * 2,
        out_specs=(pl.BlockSpec(memory_space=vm),) * 4,
        scratch_shapes=[
            vm((nz, cols, cz), F32), vm((cols, coords), F32), vm((2, coords, cols), F32),
            vm((cols, rows), F32), vm((cols, BLOCK), F32), vm((1, rows), F32), vm((1, rows), F32),
            vm((1, rows), F32), vm((rows, coords), BF16), vm((rows, coords), BF16),
            vm((cols, rows), BF16), vm((cols, rows), BF16), vm((cols, rows), BF16), vm((cols, rows), BF16),
            vm((ITERS + 1, n, 2 * nr + 8, BLOCK), F32), vm((ITERS, nz, crow, BLOCK), F32),
            vm((n, cb, rows), F32), vm((n - 1, cb, rows), F32),
            vm((cols, coords), F32), vm((nz, cols, cz), F32), vm((nz, cols, cz), F32),
            dma(nz), dma(nz), dma(ITERS + 1, n), dma(ITERS + 1, n), dma(ITERS, nz), dma(ITERS, nz),
            dma(n), dma(n), dma(nz), dma(nz),
        ],
        compiler_params=pltpu.CompilerParams(
            collective_id=0, has_side_effects=True, vmem_limit_bytes=48 << 20),
        cost_estimate=pl.CostEstimate(flops=24 * macs, bytes_accessed=16 << 20, transcendentals=9 * rows * cols),
    )(x, y, nb, db)
    return f.reshape(rows), g.reshape(cols), nt, dt


def solution(mesh):
    return jax.shard_map(
        functools.partial(on_device, mesh.shape["dp"], mesh.shape["noise"]),
        mesh=mesh,
        in_specs=(P("noise", None), P("dp", "noise"), P("noise"), P("dp")),
        out_specs=(P("noise"), P("dp"), P("dp", "noise"), P("noise", "dp")),
        check_vma=False,
    )
```

```python
import functools

import jax
import jax.numpy as jnp
from jax import lax
from jax.experimental import pallas as pl
from jax.experimental.pallas import tpu as pltpu
from jax.sharding import PartitionSpec as P

BLOCK = 128
ITERS = 3
SMOOTHING_TEMP = 0.125
TILE = 256
MESH = pl.DeviceIdType.MESH
F32 = jnp.float32
BF16 = jnp.bfloat16
NT = (((1,), (1,)), ((), ()))


def split(x):
    hi = x.astype(BF16)
    return hi, (x - hi.astype(F32)).astype(BF16)


def dot3(ahi, alo, bhi, blo):
    d = functools.partial(jnp.dot, preferred_element_type=F32)
    return d(ahi, bhi) + (d(ahi, blo) + d(alo, bhi))


def kernel(n, nz, x_ref, y_ref, nb_ref, db_ref, f_ref, g_ref, nt_ref, dt_ref,
           xs, xv, dbuf, yt, kt, gmb, fmrow, facrow, loc, xsq, xhi, xlo, whi, wlo, dhi, dlo,
           rst, cst, acc, rb, ptmp, pbuf, zbuf,
           in_s, ag_s, ag_r, rs_s, rs_r, cs_s, cs_r, h_s, h_r, zs_s, z_r):
    me = lax.axis_index("dp")
    mz = lax.axis_index("noise")
    rows, coords = x_ref.shape
    cols, cz = y_ref.shape
    nr, nc = rows // BLOCK, cols // BLOCK
    cb = coords // n
    steps = n.bit_length() - 1

    xin = pltpu.make_async_copy(x_ref, xv, in_s.at[0])
    yin = pltpu.make_async_copy(y_ref, dbuf.at[mz], in_s.at[1])
    yin.start()
    xin.start()

    barrier = pltpu.get_barrier_semaphore()
    for o in range(1, n):
        pl.semaphore_signal(barrier, inc=1, device_id={"dp": lax.rem(me + o, n)}, device_id_type=MESH)
    for o in range(1, nz):
        pl.semaphore_signal(barrier, inc=1, device_id={"noise": lax.rem(mz + o, nz)}, device_id_type=MESH)
    pl.semaphore_wait(barrier, n + nz - 2)

    def copy(src, dst, ssem, rsem, axis, to):
        return pltpu.make_async_remote_copy(
            src_ref=src, dst_ref=dst, send_sem=ssem, recv_sem=rsem,
            device_id={axis: to}, device_id_type=MESH)

    def spread(buf, ssem, rsem, axis, size, mine):
        sent = []
        for o in range(1, size):
            c = copy(buf.at[mine], buf.at[mine], ssem.at[o], rsem.at[mine], axis, lax.rem(mine + o, size))
            c.start()
            sent.append(c)
        return sent

    def arrive(buf, ssem, rsem, axis, size, mine):
        for o in range(1, size):
            src = lax.rem(mine + size - o, size)
            copy(buf.at[src], buf.at[src], ssem.at[o], rsem.at[src], axis, src).wait_recv()

    pending = []
    def ag(way, src, o):
        to = mz + 1 if way == 0 else mz - 1
        return copy(dbuf.at[src], dbuf.at[src], ag_s.at[way, o], ag_r.at[src], "noise", to)

    def has(way, o):
        return mz >= o if way == 0 else mz + o < nz

    def onward(way):
        return mz + 1 < nz if way == 0 else mz >= 1

    yin.wait()
    for way in range(2):
        @pl.when(onward(way))
        def _():
            ag(way, mz, 0).start()
    xin.wait()

    ones = jnp.ones((8, coords), F32)

    def prep(t, _):
        at = pl.ds(pl.multiple_of(t * TILE, TILE), TILE)
        x = xv[at, :]
        for k in range(nz):
            xs[k, at, :] = x[:, k * cz:(k + 1) * cz]
        hi, lo = split(x)
        xhi[at, :] = hi
        xlo[at, :] = lo
        xsq[:, at] = lax.dot_general(ones, x * x, NT, precision=lax.Precision.HIGHEST,
                                     preferred_element_type=F32)[0:1, :]
        return 0

    lax.fori_loop(0, rows // TILE, prep, 0)

    live_i = lax.broadcasted_iota(jnp.int32, (nr, BLOCK), 0) < nb_ref[0]
    live_j = lax.broadcasted_iota(jnp.int32, (nc, BLOCK), 0) < db_ref[0]
    eye = (lax.broadcasted_iota(jnp.int32, (BLOCK, BLOCK), 0)
           == lax.broadcasted_iota(jnp.int32, (BLOCK, BLOCK), 1))

    def set_gm(g):
        gm = jnp.where(live_j, g, -jnp.inf)
        for k in range(nc):
            gmb[k * BLOCK:(k + 1) * BLOCK, :] = jnp.broadcast_to(gm[k:k + 1, :], (BLOCK, BLOCK)).T

    set_gm(jnp.zeros((nc, BLOCK), F32))

    def cost(src, first):
        y = dbuf[src]
        ysq = jnp.sum(y * y, axis=1, keepdims=True)

        def body(t, _):
            at = pl.ds(pl.multiple_of(t * TILE, TILE), TILE)
            cross = lax.dot_general(y, xs[src, at, :], NT, precision=lax.Precision.HIGHEST,
                                    preferred_element_type=F32)
            if first:
                kt[:, at] = (2.0 * cross - (xsq[:, at] + ysq)) * (1.0 / SMOOTHING_TEMP)
            else:
                kt[:, at] += (2.0 * cross - ysq) * (1.0 / SMOOTHING_TEMP)
            return 0

        lax.fori_loop(0, rows // TILE, body, 0)

    cost(mz, True)
    for o in range(1, nz):
        for way in range(2):
            src = mz - o if way == 0 else mz + o

            @pl.when(has(way, o))
            def _():
                ag(way, src, o).wait_recv()

                @pl.when(onward(way))
                def _():
                    ag(way, src, o).start()

        for way in range(2):
            src = mz - o if way == 0 else mz + o

            @pl.when(has(way, o))
            def _():
                cost(src, False)

    def row_pass(r, keep):
        def body(c, _):
            at = pl.ds(pl.multiple_of(c * BLOCK, BLOCK), BLOCK)
            s = kt[:, at] + gmb[...]
            top = jnp.max(s, axis=0, keepdims=True)
            e = jnp.exp(s - top)
            rst[r, me, pl.ds(c, 1), :] = top + jnp.log(jnp.sum(e, axis=0, keepdims=True))
            if keep:
                loc[pl.ds(c, 1), :] = top
                hi, lo = split(e)
                whi[:, at] = hi
                wlo[:, at] = lo
            return 0

        lax.fori_loop(0, nr, body, 0)
        rst[r, me, nr:nr + 1, :] = jnp.full((1, BLOCK), db_ref[0].astype(F32), F32)
        return spread(rst.at[r], rs_s.at[r], rs_r.at[r], "dp", n, me)

    def col_pass(r):
        def body(k, _):
            s = kt[pl.ds(pl.multiple_of(k * BLOCK, BLOCK), BLOCK), :] + fmrow[...]
            top = jnp.max(s, axis=1, keepdims=True)
            mass = jnp.sum(jnp.exp(s - top), axis=1, keepdims=True)
            cst[r, mz, pl.ds(k, 1), :] = jnp.sum(jnp.where(eye, top + jnp.log(mass), 0.0), axis=0, keepdims=True)
            return 0

        lax.fori_loop(0, nc, body, 0)
        cst[r, mz, nc:nc + 1, :] = jnp.full((1, BLOCK), nb_ref[0].astype(F32), F32)
        return spread(cst.at[r], cs_s.at[r], cs_r.at[r], "noise", nz, mz)

    def combine(st, r, size, m):
        tops = [st[r, k, 0:m, :] for k in range(size)]
        top = functools.reduce(jnp.maximum, tops)
        mass = sum(jnp.exp(t - top) for t in tops)
        return top + jnp.log(mass)

    def log_mass(st, size, m):
        count = sum(st[0, k, m:m + 1, :] for k in range(size))
        return -jnp.log(count * float(BLOCK))

    def set_row(ref, v):
        for c in range(nr):
            ref[:, c * BLOCK:(c + 1) * BLOCK] = v[c:c + 1, :]

    log_a = log_b = f = g = None
    for turn in range(ITERS):
        pending += row_pass(turn, False)
        if turn == 0:
            full = jnp.concatenate([dbuf[k] for k in range(nz)], axis=1).T
            hi, lo = split(full)
            yt[0] = hi.astype(F32)
            yt[1] = lo.astype(F32)
        arrive(rst.at[turn], rs_s.at[turn], rs_r.at[turn], "dp", n, me)
        if turn == 0:
            log_b = log_mass(rst, n, nr)
        f = -(combine(rst, turn, n, nr) + log_b)
        set_row(fmrow, jnp.where(live_i, f, -jnp.inf))
        pending += col_pass(turn)
        arrive(cst.at[turn], cs_s.at[turn], cs_r.at[turn], "noise", nz, mz)
        if turn == 0:
            log_a = log_mass(cst, nz, nc)
        g = -(combine(cst, turn, nz, nc) + log_a)
        set_gm(g)
    f_ref[...] = jnp.where(live_i, SMOOTHING_TEMP * f, 0.0)
    g_ref[...] = jnp.where(live_j, SMOOTHING_TEMP * g, 0.0)

    pending += row_pass(ITERS, True)

    set_row(fmrow, jnp.where(live_i, f + log_a, -jnp.inf))

    def plan(c, _):
        at = pl.ds(pl.multiple_of(c * BLOCK, BLOCK), BLOCK)
        hi, lo = split(jnp.exp(kt[:, at] + fmrow[:, at] + gmb[...]))
        dhi[:, at] = hi
        dlo[:, at] = lo
        return 0

    lax.fori_loop(0, nr, plan, 0)

    def project(t, _):
        at = pl.ds(pl.multiple_of(t * TILE, TILE), TILE)
        ptmp[:, at] = dot3(dhi[...], dlo[...], xhi[:, at], xlo[:, at])
        return 0

    lax.fori_loop(0, coords // TILE, project, 0)
    for k in range(nz):
        pbuf[k] = ptmp[:, k * cz:(k + 1) * cz]

    def zsend(way, to):
        side = mz + 1 if way == 0 else mz - 1
        return copy(pbuf.at[to], zbuf.at[way, to], zs_s.at[way, to], z_r.at[way, to], "noise", side)

    rank = (mz, nz - 1 - mz)

    def target(way, t):
        return t if way == 0 else nz - 1 - t

    for way in range(2):
        @pl.when(rank[way] == 0)
        def _():
            for t in range(nz - 1, 0, -1):
                zsend(way, target(way, t)).start()

    def relay(turn):
        for way in range(2):
            t = nz - 1 - turn + rank[way]

            @pl.when((rank[way] >= 1) & (rank[way] <= turn))
            def _():
                to = target(way, t)
                zsend(way, to).wait_recv()
                pbuf[to] += zbuf[way, to]
                zsend(way, to).start()

    arrive(rst.at[ITERS], rs_s.at[ITERS], rs_r.at[ITERS], "dp", n, me)
    level = combine(rst, ITERS, n, nr)
    set_row(facrow, jnp.where(live_i, jnp.exp(loc[...] - level), 0.0))

    core = lax.rem(me, 2)

    def flip(w):
        return w * (1 - 2 * lax.rem(me // w, 2))

    delta = [flip(1)] + [(1 - core) * flip(1 << s) + core * flip(1 << (steps - s)) for s in range(1, steps)]

    def owner(q):
        d = me
        for s in range(steps):
            if (q >> s) & 1:
                d = d + delta[s]
        return d

    def landed(s, q):
        if s > 0:
            return q - (1 << s)
        return sum(1 << (steps - t) for t in range(1, steps) if (q >> t) & 1)

    slot = {}
    for s in range(steps):
        for q in range(0, n, 2 << s):
            slot[s, q] = len(slot)

    parts = 2 if rows % (2 * TILE) == 0 else 1
    wide = rows // parts

    def lows(q):
        return (q & -q) if q else n

    def half(odd, h):
        qs = list(range(odd, n, 2))
        hi = jnp.concatenate([yt[0, pl.ds(pl.multiple_of(owner(q) * cb, cb), cb), :] for q in qs], axis=0).astype(BF16)
        lo = jnp.concatenate([yt[1, pl.ds(pl.multiple_of(owner(q) * cb, cb), cb), :] for q in qs], axis=0).astype(BF16)

        def body(t, _):
            at = pl.ds(pl.multiple_of(h * wide + t * TILE, TILE), TILE)
            out = dot3(hi, lo, whi[:, at], wlo[:, at]) * facrow[:, at]
            for m, q in enumerate(qs):
                acc[q, :, at] = out[m * cb:(m + 1) * cb, :]
            return 0

        lax.fori_loop(0, wide // TILE, body, 0)

    def link(s, q, to, h):
        at = pl.ds(h * wide, wide)
        i = slot[s, to]
        return copy(acc.at[q, :, at], rb.at[i, :, at], h_s.at[q, h], h_r.at[i, h], "dp", me + delta[s])

    def hop(s, q, h):
        c = link(s, q, landed(s, q), h)
        c.start()
        pending.append(c)

    def take(s, q, h):
        link(s, q, q, h).wait_recv()
        at = pl.ds(h * wide, wide)
        acc[q, :, at] += rb[slot[s, q], :, at]

    def urgent(q):
        return (lows(q), -q)

    for h in range(parts):
        half(1, h)
        for q in sorted(range(1, n, 2), key=lambda q: urgent(landed(0, q))):
            hop(0, q, h)
    for h in range(parts):
        half(0, h)
    turn = 1
    for s in range(1, steps):
        for q in sorted(range(1 << s, n, 2 << s), key=lambda q: urgent(landed(s, q))):
            for h in range(parts):
                take(s - 1, q, h)
                hop(s, q, h)
        for q in sorted(range(0, n, 2 << s), key=urgent):
            if q == 0 or s == steps - 1:
                if turn < nz - 1:
                    relay(turn)
                    turn += 1
            for h in range(parts):
                take(s - 1, q, h)
    for late in range(turn, nz - 1):
        relay(late)

    dt_ref[...] = pbuf[mz].T
    for way in range(2):
        @pl.when(rank[way] >= 1)
        def _():
            zsend(way, mz).wait_recv()
            dt_ref[...] += zbuf[way, mz].T

    for h in range(parts):
        take(steps - 1, 0, h)
    nt_ref[...] = acc[0]
    for way in range(2):
        for o in range(nz - 1):
            @pl.when(has(way, o) & onward(way))
            def _():
                ag(way, mz - o if way == 0 else mz + o, o).wait_send()

        for t in range(1, nz):
            @pl.when(rank[way] < t)
            def _():
                zsend(way, target(way, t)).wait_send()
    for c in pending:
        c.wait_send()


def on_device(n, nz, x, y, nb, db):
    rows, coords = x.shape
    cols, cz = y.shape
    nr, nc = rows // BLOCK, cols // BLOCK
    cb = coords // n
    steps = n.bit_length() - 1
    up = lambda k: -(-k // 8) * 8
    vm = pltpu.VMEM
    dma = lambda *s: pltpu.SemaphoreType.DMA(s)
    macs = rows * cols * coords
    f, g, nt, dt = pl.pallas_call(
        functools.partial(kernel, n, nz),
        out_shape=(
            jax.ShapeDtypeStruct((nr, BLOCK), F32),
            jax.ShapeDtypeStruct((nc, BLOCK), F32),
            jax.ShapeDtypeStruct((cb, rows), F32),
            jax.ShapeDtypeStruct((cz, cols), F32),
        ),
        in_specs=[pl.BlockSpec(memory_space=pltpu.HBM)] * 2 + [pl.BlockSpec(memory_space=pltpu.SMEM)] * 2,
        out_specs=(pl.BlockSpec(memory_space=vm),) * 4,
        scratch_shapes=[
            vm((nz, rows, cz), F32), vm((rows, coords), F32), vm((nz, cols, cz), F32), vm((2, coords, cols), F32),
            vm((cols, rows), F32), vm((cols, BLOCK), F32), vm((1, rows), F32), vm((1, rows), F32),
            vm((nr, BLOCK), F32), vm((1, rows), F32), vm((rows, coords), BF16), vm((rows, coords), BF16),
            vm((cols, rows), BF16), vm((cols, rows), BF16), vm((cols, rows), BF16), vm((cols, rows), BF16),
            vm((ITERS + 1, n, up(nr + 1), BLOCK), F32), vm((ITERS, nz, up(nc + 1), BLOCK), F32),
            vm((n, cb, rows), F32), vm((n - 1, cb, rows), F32),
            vm((cols, coords), F32), vm((nz, cols, cz), F32), vm((2, nz, cols, cz), F32),
            dma(2), dma(2, nz), dma(nz), dma(ITERS + 1, n), dma(ITERS + 1, n), dma(ITERS, nz), dma(ITERS, nz),
            dma(n, 2), dma(n, 2), dma(2, nz), dma(2, nz),
        ],
        compiler_params=pltpu.CompilerParams(
            collective_id=0, has_side_effects=True, vmem_limit_bytes=56 << 20),
        cost_estimate=pl.CostEstimate(flops=24 * macs, bytes_accessed=16 << 20, transcendentals=9 * rows * cols),
    )(x, y, nb, db)
    return f.reshape(rows), g.reshape(cols), nt, dt


def solution(mesh):
    return jax.shard_map(
        functools.partial(on_device, mesh.shape["dp"], mesh.shape["noise"]),
        mesh=mesh,
        in_specs=(P("noise", None), P("dp", "noise"), P("noise"), P("dp")),
        out_specs=(P("noise"), P("dp"), P("dp", "noise"), P("noise", "dp")),
        check_vma=False,
    )
```

```python
import functools

import jax
import jax.numpy as jnp
from jax import lax
from jax.experimental import pallas as pl
from jax.experimental.pallas import tpu as pltpu
from jax.sharding import PartitionSpec as P

BLOCK = 128
ITERS = 3
SMOOTHING_TEMP = 0.125
TILE = 256
MESH = pl.DeviceIdType.MESH
F32 = jnp.float32
BF16 = jnp.bfloat16
NT = (((1,), (1,)), ((), ()))


def split(x):
    hi = x.astype(BF16)
    return hi, (x - hi.astype(F32)).astype(BF16)


def dot3(ahi, alo, bhi, blo):
    d = functools.partial(jnp.dot, preferred_element_type=F32)
    return d(ahi, bhi) + (d(ahi, blo) + d(alo, bhi))


def kernel(n, nz, x_ref, y_ref, nb_ref, db_ref, f_ref, g_ref, nt_ref, dt_ref,
           xs, xv, dbuf, yt, kt, gmb, fmrow, facrow, loc, xsq, xhi, xlo, whi, wlo, dhi, dlo,
           rst, cst, acc, rb, ptmp, pbuf, zbuf,
           in_s, ag_s, ag_r, rs_s, rs_r, cs_s, cs_r, h_s, h_r, zs_s, z_r):
    me = lax.axis_index("dp")
    mz = lax.axis_index("noise")
    rows, coords = x_ref.shape
    cols, cz = y_ref.shape
    nr, nc = rows // BLOCK, cols // BLOCK
    cb = coords // n
    steps = n.bit_length() - 1

    xin = pltpu.make_async_copy(x_ref, xv, in_s.at[0])
    yin = pltpu.make_async_copy(y_ref, dbuf.at[mz], in_s.at[1])
    yin.start()
    xin.start()

    barrier = pltpu.get_barrier_semaphore()
    for o in range(1, n):
        pl.semaphore_signal(barrier, inc=1, device_id={"dp": lax.rem(me + o, n)}, device_id_type=MESH)
    for o in range(1, nz):
        pl.semaphore_signal(barrier, inc=1, device_id={"noise": lax.rem(mz + o, nz)}, device_id_type=MESH)
    pl.semaphore_wait(barrier, n + nz - 2)

    def copy(src, dst, ssem, rsem, axis, to):
        return pltpu.make_async_remote_copy(
            src_ref=src, dst_ref=dst, send_sem=ssem, recv_sem=rsem,
            device_id={axis: to}, device_id_type=MESH)

    def spread(buf, ssem, rsem, axis, size, mine):
        sent = []
        for o in range(1, size):
            c = copy(buf.at[mine], buf.at[mine], ssem.at[o], rsem.at[mine], axis, lax.rem(mine + o, size))
            c.start()
            sent.append(c)
        return sent

    def arrive(buf, ssem, rsem, axis, size, mine):
        for o in range(1, size):
            src = lax.rem(mine + size - o, size)
            copy(buf.at[src], buf.at[src], ssem.at[o], rsem.at[src], axis, src).wait_recv()

    pending = []
    def ag(way, src, o, p):
        to = mz + 1 if way == 0 else mz - 1
        piece = dbuf.at[src, p * BLOCK:(p + 1) * BLOCK, :]
        return copy(piece, piece, ag_s.at[way, o, p], ag_r.at[src, p], "noise", to)

    def has(way, o):
        return mz >= o if way == 0 else mz + o < nz

    def onward(way):
        return mz + 1 < nz if way == 0 else mz >= 1

    yin.wait()
    for way in range(2):
        @pl.when(onward(way))
        def _():
            for p in range(nc):
                ag(way, mz, 0, p).start()
    xin.wait()

    ones = jnp.ones((8, coords), F32)

    def prep(t, _):
        at = pl.ds(pl.multiple_of(t * TILE, TILE), TILE)
        x = xv[at, :]
        for k in range(nz):
            xs[k, at, :] = x[:, k * cz:(k + 1) * cz]
        hi, lo = split(x)
        xhi[at, :] = hi
        xlo[at, :] = lo
        xsq[:, at] = lax.dot_general(ones, x * x, NT, precision=lax.Precision.HIGHEST,
                                     preferred_element_type=F32)[0:1, :]
        return 0

    lax.fori_loop(0, rows // TILE, prep, 0)

    live_i = lax.broadcasted_iota(jnp.int32, (nr, BLOCK), 0) < nb_ref[0]
    live_j = lax.broadcasted_iota(jnp.int32, (nc, BLOCK), 0) < db_ref[0]
    eye = (lax.broadcasted_iota(jnp.int32, (BLOCK, BLOCK), 0)
           == lax.broadcasted_iota(jnp.int32, (BLOCK, BLOCK), 1))

    def set_gm(g):
        gm = jnp.where(live_j, g, -jnp.inf)
        for k in range(nc):
            gmb[k * BLOCK:(k + 1) * BLOCK, :] = jnp.broadcast_to(gm[k:k + 1, :], (BLOCK, BLOCK)).T

    set_gm(jnp.zeros((nc, BLOCK), F32))

    def cost(src, first):
        y = dbuf[src]
        ysq = jnp.sum(y * y, axis=1, keepdims=True)

        def body(t, _):
            at = pl.ds(pl.multiple_of(t * TILE, TILE), TILE)
            cross = lax.dot_general(y, xs[src, at, :], NT, precision=lax.Precision.HIGHEST,
                                    preferred_element_type=F32)
            if first:
                kt[:, at] = (2.0 * cross - (xsq[:, at] + ysq)) * (1.0 / SMOOTHING_TEMP)
            else:
                kt[:, at] += (2.0 * cross - ysq) * (1.0 / SMOOTHING_TEMP)
            return 0

        lax.fori_loop(0, rows // TILE, body, 0)

    cost(mz, True)
    for o in range(1, nz):
        for p, way in [(p, way) for p in range(nc) for way in range(2)]:
            src = mz - o if way == 0 else mz + o

            @pl.when(has(way, o))
            def _():
                ag(way, src, o, p).wait_recv()

                @pl.when(onward(way))
                def _():
                    ag(way, src, o, p).start()

        for way in range(2):
            src = mz - o if way == 0 else mz + o

            @pl.when(has(way, o))
            def _():
                cost(src, False)

    def row_pass(r, keep):
        def body(c, _):
            at = pl.ds(pl.multiple_of(c * BLOCK, BLOCK), BLOCK)
            s = kt[:, at] + gmb[...]
            top = jnp.max(s, axis=0, keepdims=True)
            e = jnp.exp(s - top)
            rst[r, me, pl.ds(c, 1), :] = top + jnp.log(jnp.sum(e, axis=0, keepdims=True))
            if keep:
                loc[pl.ds(c, 1), :] = top
                hi, lo = split(e)
                whi[:, at] = hi
                wlo[:, at] = lo
            return 0

        lax.fori_loop(0, nr, body, 0)
        rst[r, me, nr:nr + 1, :] = jnp.full((1, BLOCK), db_ref[0].astype(F32), F32)
        return spread(rst.at[r], rs_s.at[r], rs_r.at[r], "dp", n, me)

    def col_pass(r):
        def body(k, _):
            s = kt[pl.ds(pl.multiple_of(k * BLOCK, BLOCK), BLOCK), :] + fmrow[...]
            top = jnp.max(s, axis=1, keepdims=True)
            mass = jnp.sum(jnp.exp(s - top), axis=1, keepdims=True)
            cst[r, mz, pl.ds(k, 1), :] = jnp.sum(jnp.where(eye, top + jnp.log(mass), 0.0), axis=0, keepdims=True)
            return 0

        lax.fori_loop(0, nc, body, 0)
        cst[r, mz, nc:nc + 1, :] = jnp.full((1, BLOCK), nb_ref[0].astype(F32), F32)
        return spread(cst.at[r], cs_s.at[r], cs_r.at[r], "noise", nz, mz)

    def combine(st, r, size, m):
        tops = [st[r, k, 0:m, :] for k in range(size)]
        top = functools.reduce(jnp.maximum, tops)
        mass = sum(jnp.exp(t - top) for t in tops)
        return top + jnp.log(mass)

    def log_mass(st, size, m):
        count = sum(st[0, k, m:m + 1, :] for k in range(size))
        return -jnp.log(count * float(BLOCK))

    def set_row(ref, v):
        for c in range(nr):
            ref[:, c * BLOCK:(c + 1) * BLOCK] = v[c:c + 1, :]

    log_a = log_b = f = g = None
    for turn in range(ITERS):
        pending += row_pass(turn, False)
        if turn == 0:
            full = jnp.concatenate([dbuf[k] for k in range(nz)], axis=1).T
            hi, lo = split(full)
            yt[0] = hi.astype(F32)
            yt[1] = lo.astype(F32)
        arrive(rst.at[turn], rs_s.at[turn], rs_r.at[turn], "dp", n, me)
        if turn == 0:
            log_b = log_mass(rst, n, nr)
        f = -(combine(rst, turn, n, nr) + log_b)
        set_row(fmrow, jnp.where(live_i, f, -jnp.inf))
        pending += col_pass(turn)
        arrive(cst.at[turn], cs_s.at[turn], cs_r.at[turn], "noise", nz, mz)
        if turn == 0:
            log_a = log_mass(cst, nz, nc)
        g = -(combine(cst, turn, nz, nc) + log_a)
        set_gm(g)
    f_ref[...] = jnp.where(live_i, SMOOTHING_TEMP * f, 0.0)
    g_ref[...] = jnp.where(live_j, SMOOTHING_TEMP * g, 0.0)

    pending += row_pass(ITERS, True)

    set_row(fmrow, jnp.where(live_i, f + log_a, -jnp.inf))

    def plan(c, _):
        at = pl.ds(pl.multiple_of(c * BLOCK, BLOCK), BLOCK)
        hi, lo = split(jnp.exp(kt[:, at] + fmrow[:, at] + gmb[...]))
        dhi[:, at] = hi
        dlo[:, at] = lo
        return 0

    lax.fori_loop(0, nr, plan, 0)

    def project(t, _):
        at = pl.ds(pl.multiple_of(t * TILE, TILE), TILE)
        ptmp[:, at] = dot3(dhi[...], dlo[...], xhi[:, at], xlo[:, at])
        return 0

    lax.fori_loop(0, coords // TILE, project, 0)
    for k in range(nz):
        pbuf[k] = ptmp[:, k * cz:(k + 1) * cz]

    def zsend(way, to):
        side = mz + 1 if way == 0 else mz - 1
        return copy(pbuf.at[to], zbuf.at[way, to], zs_s.at[way, to], z_r.at[way, to], "noise", side)

    rank = (mz, nz - 1 - mz)

    def target(way, t):
        return t if way == 0 else nz - 1 - t

    for way in range(2):
        @pl.when(rank[way] == 0)
        def _():
            for t in range(nz - 1, 0, -1):
                zsend(way, target(way, t)).start()

    def relay(turn):
        for way in range(2):
            t = nz - 1 - turn + rank[way]

            @pl.when((rank[way] >= 1) & (rank[way] <= turn))
            def _():
                to = target(way, t)
                zsend(way, to).wait_recv()
                pbuf[to] += zbuf[way, to]
                zsend(way, to).start()

    arrive(rst.at[ITERS], rs_s.at[ITERS], rs_r.at[ITERS], "dp", n, me)
    level = combine(rst, ITERS, n, nr)
    set_row(facrow, jnp.where(live_i, jnp.exp(loc[...] - level), 0.0))

    core = lax.rem(me, 2)

    def flip(w):
        return w * (1 - 2 * lax.rem(me // w, 2))

    delta = [flip(1)] + [(1 - core) * flip(1 << s) + core * flip(1 << (steps - s)) for s in range(1, steps)]

    def owner(q):
        d = me
        for s in range(steps):
            if (q >> s) & 1:
                d = d + delta[s]
        return d

    def landed(s, q):
        if s > 0:
            return q - (1 << s)
        return sum(1 << (steps - t) for t in range(1, steps) if (q >> t) & 1)

    slot = {}
    for s in range(steps):
        for q in range(0, n, 2 << s):
            slot[s, q] = len(slot)

    parts = 2 if rows % (2 * TILE) == 0 else 1
    wide = rows // parts

    def lows(q):
        return (q & -q) if q else n

    def half(odd, h):
        qs = list(range(odd, n, 2))
        hi = jnp.concatenate([yt[0, pl.ds(pl.multiple_of(owner(q) * cb, cb), cb), :] for q in qs], axis=0).astype(BF16)
        lo = jnp.concatenate([yt[1, pl.ds(pl.multiple_of(owner(q) * cb, cb), cb), :] for q in qs], axis=0).astype(BF16)

        def body(t, _):
            at = pl.ds(pl.multiple_of(h * wide + t * TILE, TILE), TILE)
            out = dot3(hi, lo, whi[:, at], wlo[:, at]) * facrow[:, at]
            for m, q in enumerate(qs):
                acc[q, :, at] = out[m * cb:(m + 1) * cb, :]
            return 0

        lax.fori_loop(0, wide // TILE, body, 0)

    def link(s, q, to, h):
        at = pl.ds(h * wide, wide)
        i = slot[s, to]
        return copy(acc.at[q, :, at], rb.at[i, :, at], h_s.at[q, h], h_r.at[i, h], "dp", me + delta[s])

    def hop(s, q, h):
        c = link(s, q, landed(s, q), h)
        c.start()
        pending.append(c)

    def take(s, q, h):
        link(s, q, q, h).wait_recv()
        at = pl.ds(h * wide, wide)
        acc[q, :, at] += rb[slot[s, q], :, at]

    def urgent(q):
        return (lows(q), -q)

    for h in range(parts):
        half(1, h)
        for q in sorted(range(1, n, 2), key=lambda q: urgent(landed(0, q))):
            hop(0, q, h)
    for h in range(parts):
        half(0, h)
    turn = 1
    for s in range(1, steps):
        for q in sorted(range(1 << s, n, 2 << s), key=lambda q: urgent(landed(s, q))):
            for h in range(parts):
                take(s - 1, q, h)
                hop(s, q, h)
        for q in sorted(range(0, n, 2 << s), key=urgent):
            for h in range(parts):
                take(s - 1, q, h)
        if turn < nz - 1:
            relay(turn)
            turn += 1
    for late in range(turn, nz - 1):
        relay(late)

    dt_ref[...] = pbuf[mz].T
    for way in range(2):
        @pl.when(rank[way] >= 1)
        def _():
            zsend(way, mz).wait_recv()
            dt_ref[...] += zbuf[way, mz].T

    for h in range(parts):
        take(steps - 1, 0, h)
    nt_ref[...] = acc[0]
    for way in range(2):
        for o in range(nz - 1):
            @pl.when(has(way, o) & onward(way))
            def _():
                for p in range(nc):
                    ag(way, mz - o if way == 0 else mz + o, o, p).wait_send()

        for t in range(1, nz):
            @pl.when(rank[way] < t)
            def _():
                zsend(way, target(way, t)).wait_send()
    for c in pending:
        c.wait_send()


def on_device(n, nz, x, y, nb, db):
    rows, coords = x.shape
    cols, cz = y.shape
    nr, nc = rows // BLOCK, cols // BLOCK
    cb = coords // n
    steps = n.bit_length() - 1
    up = lambda k: -(-k // 8) * 8
    vm = pltpu.VMEM
    dma = lambda *s: pltpu.SemaphoreType.DMA(s)
    macs = rows * cols * coords
    f, g, nt, dt = pl.pallas_call(
        functools.partial(kernel, n, nz),
        out_shape=(
            jax.ShapeDtypeStruct((nr, BLOCK), F32),
            jax.ShapeDtypeStruct((nc, BLOCK), F32),
            jax.ShapeDtypeStruct((cb, rows), F32),
            jax.ShapeDtypeStruct((cz, cols), F32),
        ),
        in_specs=[pl.BlockSpec(memory_space=pltpu.HBM)] * 2 + [pl.BlockSpec(memory_space=pltpu.SMEM)] * 2,
        out_specs=(pl.BlockSpec(memory_space=vm),) * 4,
        scratch_shapes=[
            vm((nz, rows, cz), F32), vm((rows, coords), F32), vm((nz, cols, cz), F32), vm((2, coords, cols), F32),
            vm((cols, rows), F32), vm((cols, BLOCK), F32), vm((1, rows), F32), vm((1, rows), F32),
            vm((nr, BLOCK), F32), vm((1, rows), F32), vm((rows, coords), BF16), vm((rows, coords), BF16),
            vm((cols, rows), BF16), vm((cols, rows), BF16), vm((cols, rows), BF16), vm((cols, rows), BF16),
            vm((ITERS + 1, n, up(nr + 1), BLOCK), F32), vm((ITERS, nz, up(nc + 1), BLOCK), F32),
            vm((n, cb, rows), F32), vm((n - 1, cb, rows), F32),
            vm((cols, coords), F32), vm((nz, cols, cz), F32), vm((2, nz, cols, cz), F32),
            dma(2), dma(2, nz, nc), dma(nz, nc), dma(ITERS + 1, n), dma(ITERS + 1, n), dma(ITERS, nz), dma(ITERS, nz),
            dma(n, 2), dma(n, 2), dma(2, nz), dma(2, nz),
        ],
        compiler_params=pltpu.CompilerParams(
            collective_id=0, has_side_effects=True, vmem_limit_bytes=44 << 20),
        cost_estimate=pl.CostEstimate(flops=24 * macs, bytes_accessed=16 << 20, transcendentals=9 * rows * cols),
    )(x, y, nb, db)
    return f.reshape(rows), g.reshape(cols), nt, dt


def solution(mesh):
    return jax.shard_map(
        functools.partial(on_device, mesh.shape["dp"], mesh.shape["noise"]),
        mesh=mesh,
        in_specs=(P("noise", None), P("dp", "noise"), P("noise"), P("dp")),
        out_specs=(P("noise"), P("dp"), P("dp", "noise"), P("noise", "dp")),
        check_vma=False,
    )
```

```python
import functools

import jax
import jax.numpy as jnp
from jax import lax
from jax.experimental import pallas as pl
from jax.experimental.pallas import tpu as pltpu
from jax.sharding import PartitionSpec as P

BLOCK = 128
ITERS = 3
SMOOTHING_TEMP = 0.125
TILE = 256
MESH = pl.DeviceIdType.MESH
F32 = jnp.float32
BF16 = jnp.bfloat16
NT = (((1,), (1,)), ((), ()))


def split(x):
    hi = x.astype(BF16)
    return hi, (x - hi.astype(F32)).astype(BF16)


def dot3(ahi, alo, bhi, blo):
    d = functools.partial(jnp.dot, preferred_element_type=F32)
    return d(ahi, bhi) + (d(ahi, blo) + d(alo, bhi))


def kernel(n, nz, x_ref, y_ref, nb_ref, db_ref, f_ref, g_ref, nt_ref, dt_ref,
           xs, xv, dbuf, yt, kt, gmb, fmrow, facrow, loc, xsq, xhi, xlo, whi, wlo, dhi, dlo,
           rst, cst, acc, rb, ptmp, pbuf, zbuf,
           in_s, ag_s, ag_r, rs_s, rs_r, cs_s, cs_r, h_s, h_r, zs_s, z_r):
    me = lax.axis_index("dp")
    mz = lax.axis_index("noise")
    rows, coords = x_ref.shape
    cols, cz = y_ref.shape
    nr, nc = rows // BLOCK, cols // BLOCK
    cb = coords // n
    steps = n.bit_length() - 1

    xin = pltpu.make_async_copy(x_ref, xv, in_s.at[0])
    yin = pltpu.make_async_copy(y_ref, dbuf.at[mz], in_s.at[1])
    yin.start()
    xin.start()

    barrier = pltpu.get_barrier_semaphore()
    for o in range(1, n):
        pl.semaphore_signal(barrier, inc=1, device_id={"dp": lax.rem(me + o, n)}, device_id_type=MESH)
    for o in range(1, nz):
        pl.semaphore_signal(barrier, inc=1, device_id={"noise": lax.rem(mz + o, nz)}, device_id_type=MESH)
    pl.semaphore_wait(barrier, n + nz - 2)

    def copy(src, dst, ssem, rsem, axis, to):
        return pltpu.make_async_remote_copy(
            src_ref=src, dst_ref=dst, send_sem=ssem, recv_sem=rsem,
            device_id={axis: to}, device_id_type=MESH)

    def spread(buf, ssem, rsem, axis, size, mine):
        sent = []
        for o in range(1, size):
            c = copy(buf.at[mine], buf.at[mine], ssem.at[o], rsem.at[mine], axis, lax.rem(mine + o, size))
            c.start()
            sent.append(c)
        return sent

    def arrive(buf, ssem, rsem, axis, size, mine):
        for o in range(1, size):
            src = lax.rem(mine + size - o, size)
            copy(buf.at[src], buf.at[src], ssem.at[o], rsem.at[src], axis, src).wait_recv()

    pending = []
    def ag(way, src, o, p):
        to = mz + 1 if way == 0 else mz - 1
        piece = dbuf.at[src, p * BLOCK:(p + 1) * BLOCK, :]
        return copy(piece, piece, ag_s.at[way, o, p], ag_r.at[src, p], "noise", to)

    def has(way, o):
        return mz >= o if way == 0 else mz + o < nz

    def onward(way):
        return mz + 1 < nz if way == 0 else mz >= 1

    yin.wait()
    for way in range(2):
        @pl.when(onward(way))
        def _():
            for p in range(nc):
                ag(way, mz, 0, p).start()
    xin.wait()

    ones = jnp.ones((8, coords), F32)

    def prep(t, _):
        at = pl.ds(pl.multiple_of(t * TILE, TILE), TILE)
        x = xv[at, :]
        for k in range(nz):
            xs[k, at, :] = x[:, k * cz:(k + 1) * cz]
        hi, lo = split(x)
        xhi[at, :] = hi
        xlo[at, :] = lo
        xsq[:, at] = lax.dot_general(ones, x * x, NT, precision=lax.Precision.HIGHEST,
                                     preferred_element_type=F32)[0:1, :]
        return 0

    lax.fori_loop(0, rows // TILE, prep, 0)

    live_i = lax.broadcasted_iota(jnp.int32, (nr, BLOCK), 0) < nb_ref[0]
    live_j = lax.broadcasted_iota(jnp.int32, (nc, BLOCK), 0) < db_ref[0]
    eye = (lax.broadcasted_iota(jnp.int32, (BLOCK, BLOCK), 0)
           == lax.broadcasted_iota(jnp.int32, (BLOCK, BLOCK), 1))

    def set_gm(g):
        gm = jnp.where(live_j, g, -jnp.inf)
        for k in range(nc):
            gmb[k * BLOCK:(k + 1) * BLOCK, :] = jnp.broadcast_to(gm[k:k + 1, :], (BLOCK, BLOCK)).T

    set_gm(jnp.zeros((nc, BLOCK), F32))

    def cost(src, first):
        y = dbuf[src]
        ysq = jnp.sum(y * y, axis=1, keepdims=True)

        def body(t, _):
            at = pl.ds(pl.multiple_of(t * TILE, TILE), TILE)
            cross = lax.dot_general(y, xs[src, at, :], NT, precision=lax.Precision.HIGHEST,
                                    preferred_element_type=F32)
            if first:
                kt[:, at] = (2.0 * cross - (xsq[:, at] + ysq)) * (1.0 / SMOOTHING_TEMP)
            else:
                kt[:, at] += (2.0 * cross - ysq) * (1.0 / SMOOTHING_TEMP)
            return 0

        lax.fori_loop(0, rows // TILE, body, 0)

    cost(mz, True)
    for o in range(1, nz):
        for p, way in [(p, way) for p in range(nc) for way in range(2)]:
            src = mz - o if way == 0 else mz + o

            @pl.when(has(way, o))
            def _():
                ag(way, src, o, p).wait_recv()

                @pl.when(onward(way))
                def _():
                    ag(way, src, o, p).start()

        for way in range(2):
            src = mz - o if way == 0 else mz + o

            @pl.when(has(way, o))
            def _():
                cost(src, False)

    def row_pass(r, keep):
        def body(c, _):
            at = pl.ds(pl.multiple_of(c * BLOCK, BLOCK), BLOCK)
            s = kt[:, at] + gmb[...]
            top = jnp.max(s, axis=0, keepdims=True)
            e = jnp.exp(s - top)
            rst[r, me, pl.ds(c, 1), :] = top + jnp.log(jnp.sum(e, axis=0, keepdims=True))
            if keep:
                loc[pl.ds(c, 1), :] = top
                hi, lo = split(e)
                whi[:, at] = hi
                wlo[:, at] = lo
            return 0

        lax.fori_loop(0, nr, body, 0)
        rst[r, me, nr:nr + 1, :] = jnp.full((1, BLOCK), db_ref[0].astype(F32), F32)
        return spread(rst.at[r], rs_s.at[r], rs_r.at[r], "dp", n, me)

    def col_pass(r):
        def body(k, _):
            s = kt[pl.ds(pl.multiple_of(k * BLOCK, BLOCK), BLOCK), :] + fmrow[...]
            top = jnp.max(s, axis=1, keepdims=True)
            mass = jnp.sum(jnp.exp(s - top), axis=1, keepdims=True)
            cst[r, mz, pl.ds(k, 1), :] = jnp.sum(jnp.where(eye, top + jnp.log(mass), 0.0), axis=0, keepdims=True)
            return 0

        lax.fori_loop(0, nc, body, 0)
        cst[r, mz, nc:nc + 1, :] = jnp.full((1, BLOCK), nb_ref[0].astype(F32), F32)
        return spread(cst.at[r], cs_s.at[r], cs_r.at[r], "noise", nz, mz)

    def combine(st, r, size, m):
        tops = [st[r, k, 0:m, :] for k in range(size)]
        top = functools.reduce(jnp.maximum, tops)
        mass = sum(jnp.exp(t - top) for t in tops)
        return top + jnp.log(mass)

    def log_mass(st, size, m):
        count = sum(st[0, k, m:m + 1, :] for k in range(size))
        return -jnp.log(count * float(BLOCK))

    def set_row(ref, v):
        for c in range(nr):
            ref[:, c * BLOCK:(c + 1) * BLOCK] = v[c:c + 1, :]

    log_a = log_b = f = g = None
    for turn in range(ITERS):
        pending += row_pass(turn, False)
        if turn == 0:
            full = jnp.concatenate([dbuf[k] for k in range(nz)], axis=1).T
            hi, lo = split(full)
            yt[0] = hi.astype(F32)
            yt[1] = lo.astype(F32)
        arrive(rst.at[turn], rs_s.at[turn], rs_r.at[turn], "dp", n, me)
        if turn == 0:
            log_b = log_mass(rst, n, nr)
        f = -(combine(rst, turn, n, nr) + log_b)
        set_row(fmrow, jnp.where(live_i, f, -jnp.inf))
        pending += col_pass(turn)
        arrive(cst.at[turn], cs_s.at[turn], cs_r.at[turn], "noise", nz, mz)
        if turn == 0:
            log_a = log_mass(cst, nz, nc)
        g = -(combine(cst, turn, nz, nc) + log_a)
        set_gm(g)
    f_ref[...] = jnp.where(live_i, SMOOTHING_TEMP * f, 0.0)
    g_ref[...] = jnp.where(live_j, SMOOTHING_TEMP * g, 0.0)

    pending += row_pass(ITERS, True)

    set_row(fmrow, jnp.where(live_i, f + log_a, -jnp.inf))

    def plan(c, _):
        at = pl.ds(pl.multiple_of(c * BLOCK, BLOCK), BLOCK)
        hi, lo = split(jnp.exp(kt[:, at] + fmrow[:, at] + gmb[...]))
        dhi[:, at] = hi
        dlo[:, at] = lo
        return 0

    lax.fori_loop(0, nr, plan, 0)

    def project(t, _):
        at = pl.ds(pl.multiple_of(t * TILE, TILE), TILE)
        ptmp[:, at] = dot3(dhi[...], dlo[...], xhi[:, at], xlo[:, at])
        return 0

    lax.fori_loop(0, coords // TILE, project, 0)
    for k in range(nz):
        pbuf[k] = ptmp[:, k * cz:(k + 1) * cz]

    def zsend(way, to):
        side = mz + 1 if way == 0 else mz - 1
        return copy(pbuf.at[to], zbuf.at[way, to], zs_s.at[way, to], z_r.at[way, to], "noise", side)

    rank = (mz, nz - 1 - mz)

    def target(way, t):
        return t if way == 0 else nz - 1 - t

    for way in range(2):
        @pl.when(rank[way] == 0)
        def _():
            for t in range(nz - 1, 0, -1):
                zsend(way, target(way, t)).start()

    def relay(turn):
        for way in range(2):
            t = nz - 1 - turn + rank[way]

            @pl.when((rank[way] >= 1) & (rank[way] <= turn))
            def _():
                to = target(way, t)
                zsend(way, to).wait_recv()
                pbuf[to] += zbuf[way, to]
                zsend(way, to).start()

    arrive(rst.at[ITERS], rs_s.at[ITERS], rs_r.at[ITERS], "dp", n, me)
    level = combine(rst, ITERS, n, nr)
    set_row(facrow, jnp.where(live_i, jnp.exp(loc[...] - level), 0.0))

    core = lax.rem(me, 2)

    def flip(w):
        return w * (1 - 2 * lax.rem(me // w, 2))

    delta = [flip(1)] + [(1 - core) * flip(1 << s) + core * flip(1 << (steps - s)) for s in range(1, steps)]

    def owner(q):
        d = me
        for s in range(steps):
            if (q >> s) & 1:
                d = d + delta[s]
        return d

    def landed(s, q):
        if s > 0:
            return q - (1 << s)
        return sum(1 << (steps - t) for t in range(1, steps) if (q >> t) & 1)

    slot = {}
    for s in range(steps):
        for q in range(0, n, 2 << s):
            slot[s, q] = len(slot)

    parts = 2 if rows % (2 * TILE) == 0 else 1
    wide = rows // parts

    def lows(q):
        return (q & -q) if q else n

    def half(odd, h):
        qs = list(range(odd, n, 2))
        hi = jnp.concatenate([yt[0, pl.ds(pl.multiple_of(owner(q) * cb, cb), cb), :] for q in qs], axis=0).astype(BF16)
        lo = jnp.concatenate([yt[1, pl.ds(pl.multiple_of(owner(q) * cb, cb), cb), :] for q in qs], axis=0).astype(BF16)

        def body(t, _):
            at = pl.ds(pl.multiple_of(h * wide + t * TILE, TILE), TILE)
            out = dot3(hi, lo, whi[:, at], wlo[:, at]) * facrow[:, at]
            for m, q in enumerate(qs):
                acc[q, :, at] = out[m * cb:(m + 1) * cb, :]
            return 0

        lax.fori_loop(0, wide // TILE, body, 0)

    def link(s, q, to, h):
        at = pl.ds(h * wide, wide)
        i = slot[s, to]
        return copy(acc.at[q, :, at], rb.at[i, :, at], h_s.at[q, h], h_r.at[i, h], "dp", me + delta[s])

    def hop(s, q, h):
        c = link(s, q, landed(s, q), h)
        c.start()
        pending.append(c)

    def take(s, q, h):
        link(s, q, q, h).wait_recv()
        at = pl.ds(h * wide, wide)
        acc[q, :, at] += rb[slot[s, q], :, at]

    def urgent(q):
        return (lows(q), -q)

    for h in range(parts):
        half(1, h)
        for q in sorted(range(1, n, 2), key=lambda q: urgent(landed(0, q))):
            hop(0, q, h)
    for h in range(parts):
        half(0, h)
    turn = 1
    for s in range(1, steps):
        for q in sorted(range(1 << s, n, 2 << s), key=lambda q: urgent(landed(s, q))):
            for h in range(parts):
                take(s - 1, q, h)
                hop(s, q, h)
        for q in sorted(range(0, n, 2 << s), key=urgent):
            if q == 0 or s == steps - 1:
                if turn < nz - 1:
                    relay(turn)
                    turn += 1
            for h in range(parts):
                take(s - 1, q, h)
    for late in range(turn, nz - 1):
        relay(late)

    dt_ref[...] = pbuf[mz].T
    for way in range(2):
        @pl.when(rank[way] >= 1)
        def _():
            zsend(way, mz).wait_recv()
            dt_ref[...] += zbuf[way, mz].T

    for h in range(parts):
        take(steps - 1, 0, h)
    nt_ref[...] = acc[0]
    for way in range(2):
        for o in range(nz - 1):
            @pl.when(has(way, o) & onward(way))
            def _():
                for p in range(nc):
                    ag(way, mz - o if way == 0 else mz + o, o, p).wait_send()

        for t in range(1, nz):
            @pl.when(rank[way] < t)
            def _():
                zsend(way, target(way, t)).wait_send()
    for c in pending:
        c.wait_send()


def on_device(n, nz, x, y, nb, db):
    rows, coords = x.shape
    cols, cz = y.shape
    nr, nc = rows // BLOCK, cols // BLOCK
    cb = coords // n
    steps = n.bit_length() - 1
    up = lambda k: -(-k // 8) * 8
    vm = pltpu.VMEM
    dma = lambda *s: pltpu.SemaphoreType.DMA(s)
    macs = rows * cols * coords
    f, g, nt, dt = pl.pallas_call(
        functools.partial(kernel, n, nz),
        out_shape=(
            jax.ShapeDtypeStruct((nr, BLOCK), F32),
            jax.ShapeDtypeStruct((nc, BLOCK), F32),
            jax.ShapeDtypeStruct((cb, rows), F32),
            jax.ShapeDtypeStruct((cz, cols), F32),
        ),
        in_specs=[pl.BlockSpec(memory_space=pltpu.HBM)] * 2 + [pl.BlockSpec(memory_space=pltpu.SMEM)] * 2,
        out_specs=(pl.BlockSpec(memory_space=vm),) * 4,
        scratch_shapes=[
            vm((nz, rows, cz), F32), vm((rows, coords), F32), vm((nz, cols, cz), F32), vm((2, coords, cols), F32),
            vm((cols, rows), F32), vm((cols, BLOCK), F32), vm((1, rows), F32), vm((1, rows), F32),
            vm((nr, BLOCK), F32), vm((1, rows), F32), vm((rows, coords), BF16), vm((rows, coords), BF16),
            vm((cols, rows), BF16), vm((cols, rows), BF16), vm((cols, rows), BF16), vm((cols, rows), BF16),
            vm((ITERS + 1, n, up(nr + 1), BLOCK), F32), vm((ITERS, nz, up(nc + 1), BLOCK), F32),
            vm((n, cb, rows), F32), vm((n - 1, cb, rows), F32),
            vm((cols, coords), F32), vm((nz, cols, cz), F32), vm((2, nz, cols, cz), F32),
            dma(2), dma(2, nz, nc), dma(nz, nc), dma(ITERS + 1, n), dma(ITERS + 1, n), dma(ITERS, nz), dma(ITERS, nz),
            dma(n, 2), dma(n, 2), dma(2, nz), dma(2, nz),
        ],
        compiler_params=pltpu.CompilerParams(
            collective_id=0, has_side_effects=True, vmem_limit_bytes=56 << 20),
        cost_estimate=pl.CostEstimate(flops=24 * macs, bytes_accessed=16 << 20, transcendentals=9 * rows * cols),
    )(x, y, nb, db)
    return f.reshape(rows), g.reshape(cols), nt, dt


def solution(mesh):
    return jax.shard_map(
        functools.partial(on_device, mesh.shape["dp"], mesh.shape["noise"]),
        mesh=mesh,
        in_specs=(P("noise", None), P("dp", "noise"), P("noise"), P("dp")),
        out_specs=(P("noise"), P("dp"), P("dp", "noise"), P("noise", "dp")),
        check_vma=False,
    )
```
